128 devices in a mesh: rows: 32 (over y, z, core), cols: 4 (over x).
Axes of the slice: x: 4, y: 4, z: 4, core: 2. Of those that a mesh axis runs over, the one named last changes fastest.
Arguments:
- pixels: bfloat16 [2048, 1024, 424], P('rows', 'cols'), as said below
- band_basis: bfloat16 [424, 48], replicated, may hold values from -0.3125 to 0.3125
- column_basis: bfloat16 [1024, 256], P('cols'), may hold values from -0.1875 to 0.1875
Outputs:
- gram: float32 [2048, 2048], P('rows', 'cols')
The draws below stay inside these ranges and needn't reach their ends.
Inputs may be any that keep to these rules, and one draw needn't show every extreme that they name: `pixels`: pixel spectra of the frame.
All inputs are finite; a program needn't handle non-finite values.
Results may differ from the reference program's by a relative error of at most 0.0003.
Values may be sent and summed in bfloat16 or wider, within the bound.
No kernel may reach another device: no remote copies, remote signals or barrier semaphores. Data moves between devices by JAX's collectives and lax.ppermute only.
A program may use at most 128 MiB of HBM per device.

```python
import jax
import jax.numpy as jnp

BANDS = 424
R3 = 48
R2 = 256
H = 2048
W = 1024


def draw_pixels(key, part):
    key = jax.random.fold_in(key, 11)
    key_scale, key_mix, key_mean, key_noise = jax.random.split(key, 4)
    scale_row = jnp.exp(jax.random.uniform(key_scale, (H, 1, 1), jnp.float32, jnp.log(2.0), jnp.log(2.5)))
    noise = jax.random.normal(key_noise, (H, W, BANDS), jnp.float32)
    mixing = jax.random.uniform(key_mix, (H, 1, 1), jnp.float32, 0.5, 1.5)
    spectra = jax.random.normal(key_mean, (1, W, BANDS), jnp.float32)
    values = scale_row * (mixing * spectra + noise) * 0.5
    return values.astype(jnp.bfloat16)


def shard_levels(key, shape, shards, smallest, largest):
    gain, own = 1.0, jax.random.fold_in(key, 6)
    for dim, parts in shards:
        draws = jnp.exp(jax.random.uniform(jax.random.fold_in(own, dim), (parts,), jnp.float32, smallest / len(shards), largest / len(shards)))
        gain = gain * jnp.repeat(draws, shape[dim] // parts).reshape([-1 if axis == dim else 1 for axis in range(len(shape))])
    return gain


def centred(own_key, extent, spread, reach, pieces=(), dtype=jnp.bfloat16):
    values = jax.random.normal(own_key, extent, jnp.float32) * spread
    if len(pieces) > 0:
        values = shard_levels(own_key, extent, pieces, -0.22, 0.18) * values
    return jnp.clip(values, min=-reach, max=reach).astype(dtype)


def setup_inputs(seed: int = 0) -> dict:
    keys = jax.random.split(jax.random.key(seed), 4)
    pixels = draw_pixels(jax.random.fold_in(keys[3], 71), 0)
    band_basis = centred(keys[1], (BANDS, R3), BANDS ** -0.5, 0.3125)
    column_basis = centred(keys[2], (W, R2), W ** -0.5, 0.1875, ((0, 4),))
    return {"pixels": pixels, "band_basis": band_basis, "column_basis": column_basis}


def reference(pixels, band_basis, column_basis):
    height = pixels.shape[0]
    width = pixels.shape[1]
    flat = pixels.reshape(height * width, BANDS)
    banded = jnp.dot(flat, band_basis, preferred_element_type=jnp.float32).astype(jnp.bfloat16)
    banded = banded.reshape(height, width, R3).transpose(0, 2, 1).reshape(height * R3, width)
    projected = jnp.dot(banded, column_basis, preferred_element_type=jnp.float32).astype(jnp.bfloat16)
    projected = projected.reshape(height, R3 * R2)
    gram = jnp.dot(projected, projected.T, preferred_element_type=jnp.float32)
    return gram * (1.0 / (R3 * R2))
```

```python
import functools

import jax
import jax.numpy as jnp
from jax import lax
from jax.experimental import pallas as pl
from jax.experimental.pallas import tpu as pltpu
from jax.sharding import Mesh, PartitionSpec as P

R3 = 48
R2 = 256
NX = 4
RX = R3 // NX
SCALE = 1.0 / (R3 * R2)
HB = 16
BF = jnp.bfloat16
F32 = jnp.float32
VMEM_LIMIT = 48 * 1024 * 1024


def shift(v, axis, n, by):
    return lax.ppermute(v, axis, [(i, (i + by) % n) for i in range(n)])


def params():
    return pltpu.CompilerParams(vmem_limit_bytes=VMEM_LIMIT)


def band_kernel(bt_ref, pix_ref, *rest):
    outs, (basis, stage) = rest[:NX], rest[NX:]
    x = lax.axis_index("x")

    @pl.when(pl.program_id(0) == 0)
    def _():
        basis[...] = jnp.zeros_like(basis)
        for k in range(NX):

            @pl.when(x == k)
            def _():
                for j in range(NX):
                    first = RX * ((k + j) % NX)
                    basis[16 * j : 16 * j + RX, :] = bt_ref[first : first + RX, :]

    for h in range(HB):
        banded = jnp.dot(basis[...], pix_ref[h], preferred_element_type=F32)
        for t in range(2):
            stage[t, 64 * h : 64 * (h + 1), :] = banded[:, 128 * t : 128 * (t + 1)]
    for j in range(NX):
        for r in range(RX):
            for t in range(2):
                rows = stage[t, pl.ds(16 * j + r, HB, stride=64), :]
                outs[j][r, :, 128 * t : 128 * (t + 1)] = rows.astype(BF)


def band(bt, pix):
    h, bands, c = pix.shape
    return pl.pallas_call(
        band_kernel,
        grid=(h // HB,),
        in_specs=[
            pl.BlockSpec((R3, bands), lambda i: (0, 0)),
            pl.BlockSpec((HB, bands, c), lambda i: (i, 0, 0)),
        ],
        out_specs=[pl.BlockSpec((RX, HB, c), lambda i: (0, i, 0))] * NX,
        out_shape=[jax.ShapeDtypeStruct((RX, h, c), BF)] * NX,
        scratch_shapes=[pltpu.VMEM((64, bands), BF), pltpu.VMEM((2, 64 * HB, c // 2), F32)],
        compiler_params=params(),
        cost_estimate=pl.CostEstimate(
            flops=2 * h * c * bands * 64, bytes_accessed=pix.size * 2, transcendentals=0
        ),
        name="band",
    )(bt, pix)


def column_kernel(b0, b1, b2, b3, col_ref, out_ref):
    x = lax.axis_index("x")
    cols = [col_ref[lax.rem(x + NX - j, NX)] for j in range(NX)]
    rows = b0.shape[1]
    for r in range(RX):
        total = jnp.zeros((rows, R2), F32)
        for j, b in enumerate((b0, b1, b2, b3)):
            total += jnp.dot(b[r], cols[j], preferred_element_type=F32)
        out_ref[:, R2 * r : R2 * (r + 1)] = total.astype(BF)


def column(blocks, col):
    r, h, c = blocks[0].shape
    return pl.pallas_call(
        column_kernel,
        out_shape=jax.ShapeDtypeStruct((h, r * R2), BF),
        compiler_params=params(),
        cost_estimate=pl.CostEstimate(
            flops=2 * r * h * 4 * c * R2, bytes_accessed=2 * 5 * r * h * c, transcendentals=0
        ),
        name="column",
    )(*blocks, col)


def gram_kernel(*refs):
    zs, mine, theirs, outs = refs[:4], refs[4:8], refs[8:12], refs[12:16]
    lhs, rhs, sem = refs[16:]
    x, y, core = lax.axis_index("x"), lax.axis_index("y"), lax.axis_index("core")
    n = zs[0].shape[0]
    copies = []
    for d in range(4):
        copies.append(pltpu.make_async_copy(zs[d], lhs.at[pl.ds(n * d, n)], sem.at[d]))
    for e in range(4):
        owner = lax.rem(y + e + NX - x, NX)
        for half, ref in ((core, mine[e]), (1 - core, theirs[e])):
            at = pl.multiple_of((owner * 2 + half) * n, n)
            copies.append(
                pltpu.make_async_copy(ref, rhs.at[pl.ds(at, n)], sem.at[len(copies)])
            )
    for copy in copies:
        copy.start()
    for copy in copies:
        copy.wait()
    for d in range(4):
        outs[d][...] = lax.dot_general(
            lhs[...],
            rhs[2 * n * d : 2 * n * (d + 1), :],
            (((1,), (1,)), ((), ())),
            preferred_element_type=F32,
        )


def gram(zs, mine, theirs):
    n, k = zs[0].shape
    return pl.pallas_call(
        gram_kernel,
        in_specs=[pl.BlockSpec(memory_space=pl.ANY)] * 12,
        out_shape=[jax.ShapeDtypeStruct((4 * n, 2 * n), F32)] * 4,
        scratch_shapes=[
            pltpu.VMEM((4 * n, k), BF),
            pltpu.VMEM((8 * n, k), BF),
            pltpu.SemaphoreType.DMA((12,)),
        ],
        compiler_params=params(),
        cost_estimate=pl.CostEstimate(
            flops=2 * 32 * n * n * k, bytes_accessed=2 * 12 * n * k, transcendentals=0
        ),
        name="gram",
    )(*zs, *mine, *theirs)


def sum_kernel(g0, g1, g2, g3, *outs):
    n = outs[0].shape[0]
    for d in range(4):
        at = slice(n * d, n * (d + 1))
        outs[d][...] = (g0[at, :] + g1[at, :] + g2[at, :] + g3[at, :]) * SCALE


def sum_x(parts):
    n, m = parts[0].shape
    return pl.pallas_call(
        sum_kernel,
        out_shape=[jax.ShapeDtypeStruct((n // 4, m), F32)] * 4,
        name="sum_x",
    )(*parts)


def place_kernel(p0, p1, p2, p3, out_ref):
    z = lax.axis_index("z")
    m = p0.shape[1]
    for d, p in enumerate((p0, p1, p2, p3)):
        at = pl.multiple_of(lax.rem(z + 4 - d, 4) * m, m)
        out_ref[:, pl.ds(at, m)] = p[...]


def place(parts):
    n, m = parts[0].shape
    return pl.pallas_call(
        place_kernel, out_shape=jax.ShapeDtypeStruct((n, 4 * m), F32), name="place"
    )(*parts)


def local(pixels, band_basis, column_basis):
    col = lax.all_gather(column_basis, "x", axis=0, tiled=False)
    blocks = band(band_basis.T, pixels.transpose(0, 2, 1))
    blocks = [b if j == 0 else shift(b, "x", NX, j) for j, b in enumerate(blocks)]
    mine = column(blocks, col)
    ys = [mine] + [shift(mine, "y", 4, -e) for e in range(1, 4)]
    zs = [mine] + [shift(mine, "z", 4, -e) for e in range(1, 4)]
    theirs = [shift(v, "core", 2, 1) for v in ys]
    parts = gram(zs, ys, theirs)
    parts = [g if d == 0 else shift(g, "x", NX, d) for d, g in enumerate(parts)]
    parts = sum_x(parts)
    parts = [g if d == 0 else shift(g, "z", 4, d) for d, g in enumerate(parts)]
    return place(parts)


def solution(mesh):
    inner = Mesh(mesh.devices.reshape(4, 4, 2, 4), ("y", "z", "core", "x"))
    return jax.shard_map(
        local,
        mesh=inner,
        in_specs=(P(("y", "z", "core"), "x", None), P(), P("x", None)),
        out_specs=P(("y", "z", "core"), "x"),
        check_vma=False,
    )
```

```python
import functools

import jax
import jax.numpy as jnp
from jax import lax
from jax.experimental import pallas as pl
from jax.experimental.pallas import tpu as pltpu
from jax.sharding import Mesh, PartitionSpec as P

R3 = 48
R2 = 256
N = 4
RX = R3 // N
SCALE = 1.0 / (R3 * R2)
IN_ROWS = 8
OUT_ROWS = 16
EARLY = 20_000_000_000
LATE = 100_000_000
BF = jnp.bfloat16
F32 = jnp.float32
VMEM = pl.BlockSpec(memory_space=pltpu.VMEM)


def shift(v, axis, by):
    names = ("core", "x") if axis == "x" else (axis, "core")
    index = (lambda i, c: N * c + i) if axis == "x" else (lambda i, c: 2 * i + c)
    pairs = [(index(i, c), index((i + by * (1 - 2 * c)) % N, c)) for i in range(N) for c in range(2)]
    return lax.ppermute(v, names, pairs)


def swap(v):
    return lax.ppermute(v, "core", [(0, 1), (1, 0)])


def params(mib):
    return pltpu.CompilerParams(vmem_limit_bytes=mib * 1024 * 1024)


def band_kernel(first, bt_hbm, pix_ref, *rest):
    outs, (bt_ref, basis, buf, stage, sem, bt_sem) = rest[:N], rest[N:]
    bt_copy = pltpu.make_async_copy(bt_hbm, bt_ref, bt_sem)
    bt_copy.start()
    h = outs[0].shape[1]
    copies = [
        pltpu.make_async_copy(
            pix_ref.at[pl.ds(first + IN_ROWS * g, IN_ROWS)], buf.at[pl.ds(IN_ROWS * g, IN_ROWS)], sem.at[g]
        )
        for g in range(h // IN_ROWS)
    ]
    for copy in copies:
        copy.start()
    x, core = lax.axis_index("x"), lax.axis_index("core")
    basis[...] = jnp.zeros_like(basis)
    bt_copy.wait()
    for k in range(N):
        for c in range(2):

            @pl.when((x == k) & (core == c))
            def _():
                for j in range(N):
                    at = RX * ((k + j * (1 - 2 * c)) % N)
                    basis[16 * j : 16 * j + RX, :] = bt_ref[at : at + RX, :]

    for q in range(h // OUT_ROWS):
        for i in range(OUT_ROWS):
            row = OUT_ROWS * q + i
            if row % IN_ROWS == 0:
                copies[row // IN_ROWS].wait()
            banded = jnp.dot(basis[...], buf[row], preferred_element_type=F32)
            for t in range(2):
                stage[t, 64 * i : 64 * (i + 1), :] = banded[:, 128 * t : 128 * (t + 1)]
        at = slice(OUT_ROWS * q, OUT_ROWS * (q + 1))
        for j in range(N):
            for r in range(RX):
                for t in range(2):
                    rows = stage[t, pl.ds(16 * j + r, OUT_ROWS, stride=64), :]
                    outs[j][r, at, 128 * t : 128 * (t + 1)] = rows.astype(BF)


def band(bt, pix, first, h):
    _, bands, c = pix.shape
    return pl.pallas_call(
        functools.partial(band_kernel, first),
        in_specs=[pl.BlockSpec(memory_space=pl.ANY)] * 2,
        out_specs=[VMEM] * N,
        out_shape=[jax.ShapeDtypeStruct((RX, h, c), BF)] * N,
        scratch_shapes=[
            pltpu.VMEM((R3, bands), BF),
            pltpu.VMEM((64, bands), BF),
            pltpu.VMEM((h, bands, c), BF),
            pltpu.VMEM((2, 64 * OUT_ROWS, c // 2), F32),
            pltpu.SemaphoreType.DMA((h // IN_ROWS,)),
            pltpu.SemaphoreType.DMA,
        ],
        compiler_params=params(48),
        cost_estimate=pl.CostEstimate(
            flops=2 * h * c * bands * 256, bytes_accessed=h * c * bands * 2, transcendentals=0
        ),
        name="band",
    )(bt, pix)


def column_kernel(*refs):
    blocks, cols, out_ref = refs[:N], refs[N : 2 * N], refs[2 * N]
    r, h, c = blocks[0].shape
    total = jnp.zeros((r * h, R2), F32)
    for b, col in zip(blocks, cols):
        total += jnp.dot(b[...].reshape(r * h, c), col[...], preferred_element_type=F32)
    for i in range(r):
        out_ref[:, R2 * i : R2 * (i + 1)] = total[h * i : h * (i + 1), :].astype(BF)


def column(blocks, cols, flops):
    r, h, c = blocks[0].shape
    return pl.pallas_call(
        column_kernel,
        in_specs=[VMEM] * (2 * N),
        out_specs=VMEM,
        out_shape=jax.ShapeDtypeStruct((h, r * R2), BF),
        compiler_params=params(8),
        cost_estimate=pl.CostEstimate(
            flops=flops, bytes_accessed=2 * 5 * r * h * c, transcendentals=0
        ),
        name="column",
    )(*blocks, *cols)


def gram_kernel(zs, ys, early, late, *refs):
    outs, rhs = refs[:N], refs[N]
    x, y, core = lax.axis_index("x"), lax.axis_index("y"), lax.axis_index("core")
    n = zs.shape[0] // N
    for d in range(N):
        owner = lax.rem((1 - 2 * core) * (y - x) + d + N, N)
        theirs = (early, 0) if d in (0, 3) else (late, 2)
        for half, (block, base), e in ((core, (ys, 0), d), (1 - core, theirs, (N - d) % N)):
            e -= base
            at = pl.multiple_of((owner * 2 + half) * n, n)
            rhs[pl.ds(at, n), :] = block[n * e : n * (e + 1), :]
    for d in range(N):
        outs[d][...] = lax.dot_general(
            zs[...],
            rhs[2 * n * d : 2 * n * (d + 1), :],
            (((1,), (1,)), ((), ())),
            preferred_element_type=F32,
        )


def gram(zs, ys, early, late):
    n, k = zs.shape
    return pl.pallas_call(
        gram_kernel,
        in_specs=[VMEM] * 4,
        out_specs=[VMEM] * N,
        out_shape=[jax.ShapeDtypeStruct((n, n // 2), F32)] * N,
        scratch_shapes=[pltpu.VMEM((2 * n, k), BF)],
        compiler_params=params(12),
        cost_estimate=pl.CostEstimate(
            flops=4 * n * n * k, bytes_accessed=2 * 3 * n * k, transcendentals=0
        ),
        name="gram",
    )(zs, ys, early, late)


def sum_kernel(g0, g1, g2, g3, *outs):
    n = outs[0].shape[0]
    for d in range(N):
        at = slice(n * d, n * (d + 1))
        outs[d][...] = (g0[at, :] + g1[at, :] + g2[at, :] + g3[at, :]) * SCALE


def sum_x(parts):
    n, m = parts[0].shape
    return pl.pallas_call(
        sum_kernel,
        in_specs=[VMEM] * N,
        out_specs=[VMEM] * N,
        out_shape=[jax.ShapeDtypeStruct((n // N, m), F32)] * N,
        compiler_params=params(2),
        name="sum_x",
    )(*parts)


def place_kernel(*refs):
    parts, out_ref = refs[:N], refs[N]
    z, core = lax.axis_index("z"), lax.axis_index("core")
    m = parts[0].shape[1]
    for d, part in enumerate(parts):
        at = pl.multiple_of(lax.rem(z - (1 - 2 * core) * d + N, N) * m, m)
        out_ref[:, pl.ds(at, m)] = part[...]


def place(parts):
    n, m = parts[0].shape
    return pl.pallas_call(
        place_kernel,
        in_specs=[VMEM] * N,
        out_shape=jax.ShapeDtypeStruct((n, N * m), F32),
        compiler_params=params(2),
        name="place",
    )(*parts)


def spread(parts, axis):
    return [parts[0]] + [shift(parts[d], axis, d) for d in range(1, N)]


def local(pixels, band_basis, column_basis):
    pix, bt = pixels.transpose(0, 2, 1), band_basis.T
    h = pix.shape[0] // 2
    near = shift(column_basis, "x", 1)
    first = band(bt, pix, 0, h)
    first, near = lax.optimization_barrier((first, near))
    cols = [column_basis, near, shift(near, "x", 1), swap(near)]
    first = spread(first, "x")
    second = list(band(bt, pix, h, h))
    first, second[0] = lax.optimization_barrier((first, second[0]))
    second = spread(second, "x")
    mine = [column(first, cols, EARLY)]
    up = [[shift(mine[0], axis, -1)] for axis in "yz"]
    second, up = lax.optimization_barrier((second, up))
    mine.append(column(second, cols, LATE))
    far = [[shift(up[i][0], axis, -1)] for i, axis in enumerate("yz")]
    whole = jnp.concatenate(mine, axis=0)
    for i, axis in enumerate("yz"):
        up[i].append(shift(mine[1], axis, -1))
    for i, axis in enumerate("yz"):
        far[i].append(shift(up[i][1], axis, -1))
    down = [shift(whole, axis, 1) for axis in "yz"]
    early = swap(jnp.concatenate(mine + up[0], axis=0))
    early, far, down = lax.optimization_barrier((early, far, down))
    late = jnp.concatenate(far[0] + [down[0]], axis=0)
    ys = jnp.concatenate(mine + up[0] + [late], axis=0)
    zs = jnp.concatenate(mine + up[1] + far[1] + [down[1]], axis=0)
    parts = sum_x(spread(gram(zs, ys, early, swap(late)), "x"))
    return place(spread(parts, "z"))


def solution(mesh):
    inner = Mesh(mesh.devices.reshape(4, 4, 2, 4), ("y", "z", "core", "x"))
    return jax.shard_map(
        local,
        mesh=inner,
        in_specs=(P(("y", "z", "core"), "x", None), P(), P("x", None)),
        out_specs=P(("y", "z", "core"), "x"),
        check_vma=False,
    )
```

```python
import functools

import jax
import jax.numpy as jnp
from jax import lax
from jax.experimental import pallas as pl
from jax.experimental.pallas import tpu as pltpu
from jax.sharding import Mesh, PartitionSpec as P

R3 = 48
R2 = 256
N = 4
RX = R3 // N
SCALE = 1.0 / (R3 * R2)
IN_ROWS = 8
OUT_ROWS = 16
EARLY = 20_000_000_000
LATE = 100_000_000
BF = jnp.bfloat16
F32 = jnp.float32
VMEM = pl.BlockSpec(memory_space=pltpu.VMEM)


def shift(v, axis, by):
    names = ("core", "x") if axis == "x" else (axis, "core")
    index = (lambda i, c: N * c + i) if axis == "x" else (lambda i, c: 2 * i + c)
    pairs = [(index(i, c), index((i + by * (1 - 2 * c)) % N, c)) for i in range(N) for c in range(2)]
    return lax.ppermute(v, names, pairs)


def turn(v, by):
    return lax.ppermute(v, "x", [(i, (i + by) % N) for i in range(N)])


def swap(v):
    return lax.ppermute(v, "core", [(0, 1), (1, 0)])


def params(mib):
    return pltpu.CompilerParams(vmem_limit_bytes=mib * 1024 * 1024)


def project_rows(first, basis, col, pix_ref, outs, buf, banded, stage, sem, prepare):
    h = outs[0].shape[1]
    copies = [
        pltpu.make_async_copy(
            pix_ref.at[pl.ds(first + IN_ROWS * g, IN_ROWS)], buf.at[pl.ds(IN_ROWS * g, IN_ROWS)], sem.at[g]
        )
        for g in range(h // IN_ROWS)
    ]
    for copy in copies:
        copy.start()
    prepare()
    for q in range(h // OUT_ROWS):
        for i in range(OUT_ROWS):
            row = OUT_ROWS * q + i
            if row % IN_ROWS == 0:
                copies[row // IN_ROWS].wait()
            values = jnp.dot(basis[...], buf[row], preferred_element_type=F32)
            banded[64 * i : 64 * (i + 1), :] = values.astype(BF)
        terms = jnp.dot(banded[...], col[...], preferred_element_type=F32)
        for t in range(2):
            stage[t] = terms[:, 128 * t : 128 * (t + 1)]
        at = slice(OUT_ROWS * q, OUT_ROWS * (q + 1))
        for j in range(N):
            for r in range(RX):
                for t in range(2):
                    rows = stage[t, pl.ds(16 * j + r, OUT_ROWS, stride=64), :]
                    outs[j][r, at, 128 * t : 128 * (t + 1)] = rows.astype(BF)


def first_kernel(bt_hbm, col_hbm, pix_ref, *rest):
    outs, (basis, col, bt, buf, banded, stage, sem, bt_sem, col_sem) = rest[:N], rest[N:]
    bt_copy = pltpu.make_async_copy(bt_hbm, bt, bt_sem)
    col_copy = pltpu.make_async_copy(col_hbm, col, col_sem)
    bt_copy.start()
    col_copy.start()

    def prepare():
        x = lax.axis_index("x")
        basis[...] = jnp.zeros_like(basis)
        bt_copy.wait()
        for k in range(N):

            @pl.when(x == k)
            def _():
                for j in range(N):
                    at = RX * ((k + j) % N)
                    basis[16 * j : 16 * j + RX, :] = bt[at : at + RX, :]

        col_copy.wait()

    project_rows(0, basis, col, pix_ref, outs, buf, banded, stage, sem, prepare)


def second_kernel(first, basis, col, pix_ref, *rest):
    outs, (buf, banded, stage, sem) = rest[:N], rest[N:]
    project_rows(first, basis, col, pix_ref, outs, buf, banded, stage, sem, lambda: None)


ANY = pl.BlockSpec(memory_space=pl.ANY)


def project_specs(h, bands, c):
    terms = [jax.ShapeDtypeStruct((RX, h, R2), BF)] * N
    scratch = [
        pltpu.VMEM((h, bands, c), BF),
        pltpu.VMEM((64 * OUT_ROWS, c), BF),
        pltpu.VMEM((2, 64 * OUT_ROWS, R2 // 2), F32),
        pltpu.SemaphoreType.DMA((h // IN_ROWS,)),
    ]
    common = dict(
        compiler_params=params(48),
        cost_estimate=pl.CostEstimate(
            flops=2 * h * c * bands * 256, bytes_accessed=h * c * bands * 2, transcendentals=0
        ),
    )
    return terms, scratch, common


def project_first(bt, col, pix, h):
    _, bands, c = pix.shape
    terms, scratch, common = project_specs(h, bands, c)
    kept = [jax.ShapeDtypeStruct((64, bands), BF), jax.ShapeDtypeStruct(col.shape, BF)]
    out = pl.pallas_call(
        first_kernel,
        in_specs=[ANY] * 3,
        out_specs=[VMEM] * (N + 2),
        out_shape=terms + kept,
        scratch_shapes=[pltpu.VMEM(bt.shape, BF)] + scratch + [pltpu.SemaphoreType.DMA] * 2,
        name="project_first",
        **common,
    )(bt, col, pix)
    return list(out[:N]), out[N], out[N + 1]


def project_second(basis, col, pix, first, h):
    _, bands, c = pix.shape
    terms, scratch, common = project_specs(h, bands, c)
    return list(
        pl.pallas_call(
            functools.partial(second_kernel, first),
            in_specs=[VMEM, VMEM, ANY],
            out_specs=[VMEM] * N,
            out_shape=terms,
            scratch_shapes=scratch,
            name="project_second",
            **common,
        )(basis, col, pix)
    )


def collect_kernel(*refs):
    terms, out_ref = refs[:N], refs[N]
    for r in range(RX):
        total = sum(term[r].astype(F32) for term in terms)
        out_ref[:, R2 * r : R2 * (r + 1)] = total.astype(BF)


def collect(terms, flops):
    r, h, s = terms[0].shape
    return pl.pallas_call(
        collect_kernel,
        in_specs=[VMEM] * N,
        out_specs=VMEM,
        out_shape=jax.ShapeDtypeStruct((h, r * s), BF),
        compiler_params=params(8),
        cost_estimate=pl.CostEstimate(flops=flops, bytes_accessed=2 * 5 * r * h * s, transcendentals=0),
        name="collect",
    )(*terms)


def gram_kernel(zs, ys, early, late, *refs):
    outs, rhs = refs[:N], refs[N]
    x, y, core = lax.axis_index("x"), lax.axis_index("y"), lax.axis_index("core")
    n = zs.shape[0] // N
    for d in range(N):
        owner = lax.rem((1 - 2 * core) * (y - x) + d + N, N)
        theirs = (early, 0) if d in (0, 3) else (late, 2)
        for half, (block, base), e in ((core, (ys, 0), d), (1 - core, theirs, (N - d) % N)):
            e -= base
            at = pl.multiple_of((owner * 2 + half) * n, n)
            rhs[pl.ds(at, n), :] = block[n * e : n * (e + 1), :]
    for d in range(0, N, 2):
        pair = lax.dot_general(
            zs[...],
            rhs[2 * n * d : 2 * n * (d + 2), :],
            (((1,), (1,)), ((), ())),
            preferred_element_type=F32,
        )
        outs[d][...] = pair[:, : 2 * n]
        outs[d + 1][...] = pair[:, 2 * n :]


def gram(zs, ys, early, late):
    n, k = zs.shape
    return pl.pallas_call(
        gram_kernel,
        in_specs=[VMEM] * 4,
        out_specs=[VMEM] * N,
        out_shape=[jax.ShapeDtypeStruct((n, n // 2), F32)] * N,
        scratch_shapes=[pltpu.VMEM((2 * n, k), BF)],
        compiler_params=params(12),
        cost_estimate=pl.CostEstimate(
            flops=4 * n * n * k, bytes_accessed=2 * 3 * n * k, transcendentals=0
        ),
        name="gram",
    )(zs, ys, early, late)


def sum_kernel(g0, g1, g2, g3, *outs):
    n = outs[0].shape[0]
    for d in range(N):
        at = slice(n * d, n * (d + 1))
        outs[d][...] = (g0[at, :] + g1[at, :] + g2[at, :] + g3[at, :]) * SCALE


def sum_x(parts):
    n, m = parts[0].shape
    return pl.pallas_call(
        sum_kernel,
        in_specs=[VMEM] * N,
        out_specs=[VMEM] * N,
        out_shape=[jax.ShapeDtypeStruct((n // N, m), F32)] * N,
        compiler_params=params(2),
        name="sum_x",
    )(*parts)


def place_kernel(*refs):
    parts, out_ref = refs[:N], refs[N]
    z, core = lax.axis_index("z"), lax.axis_index("core")
    m = parts[0].shape[1]
    for d, part in enumerate(parts):
        at = pl.multiple_of(lax.rem(z - (1 - 2 * core) * d + N, N) * m, m)
        out_ref[:, pl.ds(at, m)] = part[...]


def place(parts):
    n, m = parts[0].shape
    return pl.pallas_call(
        place_kernel,
        in_specs=[VMEM] * N,
        out_shape=jax.ShapeDtypeStruct((n, N * m), F32),
        compiler_params=params(2),
        name="place",
    )(*parts)


def spread(parts, axis):
    return [parts[0]] + [shift(parts[d], axis, d) for d in range(1, N)]


def local(pixels, band_basis, column_basis):
    pix, bt = pixels.transpose(0, 2, 1), band_basis.T
    h = pix.shape[0] // 2
    first, basis, col = project_first(bt, column_basis, pix, h)
    first = [first[0]] + [turn(first[j], j) for j in (1, 3, 2)]
    second = project_second(basis, col, pix, h, h)
    first, second[0] = lax.optimization_barrier((first, second[0]))
    second = [second[0]] + [turn(second[j], j) for j in (1, 3, 2)]
    mine = [collect(first, EARLY)]
    up = [[shift(mine[0], axis, -1)] for axis in "yz"]
    second, up = lax.optimization_barrier((second, up))
    mine.append(collect(second, LATE))
    far = [[shift(up[i][0], axis, -1)] for i, axis in enumerate("yz")]
    whole = jnp.concatenate(mine, axis=0)
    for i, axis in enumerate("yz"):
        up[i].append(shift(mine[1], axis, -1))
    for i, axis in enumerate("yz"):
        far[i].append(shift(up[i][1], axis, -1))
    down = [shift(whole, axis, 1) for axis in "yz"]
    early = swap(jnp.concatenate(mine + up[0], axis=0))
    early, far, down = lax.optimization_barrier((early, far, down))
    late = jnp.concatenate(far[0] + [down[0]], axis=0)
    ys = jnp.concatenate(mine + up[0] + [late], axis=0)
    zs = jnp.concatenate(mine + up[1] + far[1] + [down[1]], axis=0)
    parts = sum_x(spread(gram(zs, ys, early, swap(late)), "x"))
    return place(spread(parts, "z"))


def solution(mesh):
    inner = Mesh(mesh.devices.reshape(4, 4, 2, 4), ("y", "z", "core", "x"))
    return jax.shard_map(
        local,
        mesh=inner,
        in_specs=(P(("y", "z", "core"), "x", None), P(), P("x", None)),
        out_specs=P(("y", "z", "core"), "x"),
        check_vma=False,
    )
```

```python
import functools

import jax
import jax.numpy as jnp
from jax import lax
from jax.experimental import pallas as pl
from jax.experimental.pallas import tpu as pltpu
from jax.sharding import Mesh, PartitionSpec as P

R3 = 48
R2 = 256
N = 4
RX = R3 // N
SCALE = 1.0 / (R3 * R2)
IN_ROWS = 8
OUT_ROWS = 16
EARLY = 20_000_000_000
LATE = 100_000_000
BF = jnp.bfloat16
F32 = jnp.float32
ORDER = (0, 2, 1, 3)
VMEM = pl.BlockSpec(memory_space=pltpu.VMEM)


def shift(v, axis, by):
    names = ("core", "x") if axis == "x" else (axis, "core")
    index = (lambda i, c: N * c + i) if axis == "x" else (lambda i, c: 2 * i + c)
    pairs = [(index(i, c), index((i + by * (1 - 2 * c)) % N, c)) for i in range(N) for c in range(2)]
    return lax.ppermute(v, names, pairs)


def turn(v, by):
    return lax.ppermute(v, "x", [(i, (i + by) % N) for i in range(N)])


def swap(v):
    return lax.ppermute(v, "core", [(0, 1), (1, 0)])


def params(mib):
    return pltpu.CompilerParams(vmem_limit_bytes=mib * 1024 * 1024)


def project_rows(first, basis, col, pix_ref, outs, buf, banded, stage, sem, prepare):
    h = outs[0].shape[1]
    copies = [
        pltpu.make_async_copy(
            pix_ref.at[pl.ds(first + IN_ROWS * g, IN_ROWS)], buf.at[pl.ds(IN_ROWS * g, IN_ROWS)], sem.at[g]
        )
        for g in range(h // IN_ROWS)
    ]
    for copy in copies:
        copy.start()
    prepare()
    for q in range(h // OUT_ROWS):
        for i in range(OUT_ROWS):
            row = OUT_ROWS * q + i
            if row % IN_ROWS == 0:
                copies[row // IN_ROWS].wait()
            values = jnp.dot(basis[...], buf[row], preferred_element_type=F32)
            banded[64 * i : 64 * (i + 1), :] = values.astype(BF)
        terms = jnp.dot(banded[...], col[...], preferred_element_type=F32)
        for t in range(2):
            stage[t] = terms[:, 128 * t : 128 * (t + 1)]
        at = slice(OUT_ROWS * q, OUT_ROWS * (q + 1))
        for j in range(N):
            for r in range(RX):
                for t in range(2):
                    rows = stage[t, pl.ds(16 * j + r, OUT_ROWS, stride=64), :]
                    outs[j][r, at, 128 * t : 128 * (t + 1)] = rows.astype(outs[j].dtype)


def first_kernel(bt_hbm, col_hbm, pix_ref, *rest):
    outs, (basis, col, bt, buf, banded, stage, sem, bt_sem, col_sem) = rest[:N], rest[N:]
    bt_copy = pltpu.make_async_copy(bt_hbm, bt, bt_sem)
    col_copy = pltpu.make_async_copy(col_hbm, col, col_sem)
    bt_copy.start()
    col_copy.start()

    def prepare():
        x = lax.axis_index("x")
        basis[...] = jnp.zeros_like(basis)
        bt_copy.wait()
        for k in range(N):

            @pl.when(x == k)
            def _():
                for j in range(N):
                    at = RX * ((k + j) % N)
                    basis[16 * j : 16 * j + RX, :] = bt[at : at + RX, :]

        col_copy.wait()

    project_rows(0, basis, col, pix_ref, outs, buf, banded, stage, sem, prepare)


def second_kernel(first, basis, col, pix_ref, *rest):
    outs, (buf, banded, stage, sem) = rest[:N], rest[N:]
    project_rows(first, basis, col, pix_ref, outs, buf, banded, stage, sem, lambda: None)


ANY = pl.BlockSpec(memory_space=pl.ANY)


def project_specs(h, bands, c):
    terms = [jax.ShapeDtypeStruct((RX, h, R2), BF if j else F32) for j in range(N)]
    scratch = [
        pltpu.VMEM((h, bands, c), BF),
        pltpu.VMEM((64 * OUT_ROWS, c), BF),
        pltpu.VMEM((2, 64 * OUT_ROWS, R2 // 2), F32),
        pltpu.SemaphoreType.DMA((h // IN_ROWS,)),
    ]
    common = dict(
        compiler_params=params(48),
        cost_estimate=pl.CostEstimate(
            flops=2 * h * c * bands * 256, bytes_accessed=h * c * bands * 2, transcendentals=0
        ),
    )
    return terms, scratch, common


def project_first(bt, col, pix, h):
    _, bands, c = pix.shape
    terms, scratch, common = project_specs(h, bands, c)
    kept = [jax.ShapeDtypeStruct((64, bands), BF), jax.ShapeDtypeStruct(col.shape, BF)]
    out = pl.pallas_call(
        first_kernel,
        in_specs=[ANY] * 3,
        out_specs=[VMEM] * (N + 2),
        out_shape=terms + kept,
        scratch_shapes=[pltpu.VMEM(bt.shape, BF)] + scratch + [pltpu.SemaphoreType.DMA] * 2,
        name="project_first",
        **common,
    )(bt, col, pix)
    return list(out[:N]), out[N], out[N + 1]


def project_second(basis, col, pix, first, h):
    _, bands, c = pix.shape
    terms, scratch, common = project_specs(h, bands, c)
    return list(
        pl.pallas_call(
            functools.partial(second_kernel, first),
            in_specs=[VMEM, VMEM, ANY],
            out_specs=[VMEM] * N,
            out_shape=terms,
            scratch_shapes=scratch,
            name="project_second",
            **common,
        )(basis, col, pix)
    )


def collect_kernel(*refs):
    terms, out_ref = refs[:N], refs[N]
    for r in range(RX):
        total = sum(term[r].astype(F32) for term in terms)
        out_ref[:, R2 * r : R2 * (r + 1)] = total.astype(BF)


def collect(terms, flops):
    r, h, s = terms[0].shape
    return pl.pallas_call(
        collect_kernel,
        in_specs=[VMEM] * N,
        out_specs=VMEM,
        out_shape=jax.ShapeDtypeStruct((h, r * s), BF),
        compiler_params=params(8),
        cost_estimate=pl.CostEstimate(flops=flops, bytes_accessed=2 * 5 * r * h * s, transcendentals=0),
        name="collect",
    )(*terms)


def gram_kernel(zs, ys, early, late, *refs):
    outs, rhs = refs[:N], refs[N]
    x, y, core = lax.axis_index("x"), lax.axis_index("y"), lax.axis_index("core")
    n = zs.shape[0] // N
    for d in range(N):
        owner = lax.rem((1 - 2 * core) * (y - x) + d + N, N)
        theirs = (early, 0) if d in (0, 3) else (late, 2)
        for half, (block, base), e in ((core, (ys, 0), d), (1 - core, theirs, (N - d) % N)):
            e -= base
            at = pl.multiple_of((owner * 2 + half) * n, n)
            rhs[pl.ds(at, n), :] = block[n * e : n * (e + 1), :]
    for d in range(0, N, 2):
        pair = lax.dot_general(
            zs[...],
            rhs[2 * n * d : 2 * n * (d + 2), :],
            (((1,), (1,)), ((), ())),
            preferred_element_type=F32,
        )
        outs[d][...] = pair[:, : 2 * n]
        outs[d + 1][...] = pair[:, 2 * n :]


def gram(zs, ys, early, late):
    n, k = zs.shape
    return pl.pallas_call(
        gram_kernel,
        in_specs=[VMEM] * 4,
        out_specs=[VMEM] * N,
        out_shape=[jax.ShapeDtypeStruct((n, n // 2), F32)] * N,
        scratch_shapes=[pltpu.VMEM((2 * n, k), BF)],
        compiler_params=params(12),
        cost_estimate=pl.CostEstimate(
            flops=4 * n * n * k, bytes_accessed=2 * 3 * n * k, transcendentals=0
        ),
        name="gram",
    )(zs, ys, early, late)


def sum_kernel(g0, g1, g2, g3, *outs):
    n = outs[0].shape[0]
    for d in range(N):
        at = slice(n * d, n * (d + 1))
        outs[d][...] = (g0[at, :] + g1[at, :] + g2[at, :] + g3[at, :]) * SCALE


def sum_x(parts):
    n, m = parts[0].shape
    return pl.pallas_call(
        sum_kernel,
        in_specs=[VMEM] * N,
        out_specs=[VMEM] * N,
        out_shape=[jax.ShapeDtypeStruct((n // N, m), F32)] * N,
        compiler_params=params(2),
        name="sum_x",
    )(*parts)


def place_kernel(*refs):
    parts, out_ref = refs[:N], refs[N]
    z, core = lax.axis_index("z"), lax.axis_index("core")
    m = parts[0].shape[1]
    for d, part in zip(ORDER, parts):
        at = pl.multiple_of(lax.rem(z - (1 - 2 * core) * d + N, N) * m, m)
        out_ref[:, pl.ds(at, m)] = part[...]


def place(parts):
    n, m = parts[0].shape
    return pl.pallas_call(
        place_kernel,
        in_specs=[VMEM] * N,
        out_shape=jax.ShapeDtypeStruct((n, N * m), F32),
        compiler_params=params(2),
        name="place",
    )(*parts)


def spread(parts, axis):
    return [parts[0]] + [shift(parts[d], axis, d) for d in range(1, N)]


def local(pixels, band_basis, column_basis):
    pix, bt = pixels.transpose(0, 2, 1), band_basis.T
    h = pix.shape[0] // 2
    first, basis, col = project_first(bt, column_basis, pix, h)
    first = [first[0]] + [turn(first[j], j) for j in (1, 3, 2)]
    second = project_second(basis, col, pix, h, h)
    first, second[0] = lax.optimization_barrier((first, second[0]))
    second = [second[0]] + [turn(second[j], j) for j in (1, 3, 2)]
    mine = [collect(first, EARLY)]
    up = [[shift(mine[0], axis, -1)] for axis in "yz"]
    second, up = lax.optimization_barrier((second, up))
    mine.append(collect(second, LATE))
    for i, axis in enumerate("yz"):
        up[i].append(shift(mine[1], axis, -1))
    later = mine
    far = [shift(jnp.concatenate(up[i], axis=0), axis, -1) for i, axis in enumerate("yz")]
    down = [shift(jnp.concatenate(later, axis=0), axis, 1) for axis in "yz"]
    early = swap(jnp.concatenate(mine + up[0], axis=0))
    early, far, down = lax.optimization_barrier((early, far, down))
    late = jnp.concatenate([far[0], down[0]], axis=0)
    ys = jnp.concatenate(mine + up[0] + [late], axis=0)
    zs = jnp.concatenate(mine + up[1] + [far[1], down[1]], axis=0)
    parts = spread(gram(zs, ys, early, swap(late)), "x")
    parts = sum_x([parts[d] for d in ORDER])
    parts = spread(parts, "z")
    return place([parts[d] for d in ORDER])


def solution(mesh):
    inner = Mesh(mesh.devices.reshape(4, 4, 2, 4), ("y", "z", "core", "x"))
    return jax.shard_map(
        local,
        mesh=inner,
        in_specs=(P(("y", "z", "core"), "x", None), P(), P("x", None)),
        out_specs=P(("y", "z", "core"), "x"),
        check_vma=False,
    )
```

```python
import functools

import jax
import jax.numpy as jnp
from jax import lax
from jax.experimental import pallas as pl
from jax.experimental.pallas import tpu as pltpu
from jax.sharding import Mesh, PartitionSpec as P

R3 = 48
R2 = 256
N = 4
RX = R3 // N
SCALE = 1.0 / (R3 * R2)
IN_ROWS = 8
OUT_ROWS = 16
EARLY = 20_000_000_000
LATE = 100_000_000
BF = jnp.bfloat16
F32 = jnp.float32
ORDER = (0, 2, 1, 3)
VMEM = pl.BlockSpec(memory_space=pltpu.VMEM)


def shift(v, axis, by):
    names = ("core", "x") if axis == "x" else (axis, "core")
    index = (lambda i, c: N * c + i) if axis == "x" else (lambda i, c: 2 * i + c)
    pairs = [(index(i, c), index((i + by * (1 - 2 * c)) % N, c)) for i in range(N) for c in range(2)]
    return lax.ppermute(v, names, pairs)


def turn(v, by):
    return lax.ppermute(v, "x", [(i, (i + by) % N) for i in range(N)])


def swap(v):
    return lax.ppermute(v, "core", [(0, 1), (1, 0)])


def params(mib):
    return pltpu.CompilerParams(vmem_limit_bytes=mib * 1024 * 1024)


def project_rows(first, basis, col, pix_ref, outs, buf, banded, stage, sem, prepare):
    h = outs[0].shape[1]
    copies = [
        pltpu.make_async_copy(
            pix_ref.at[pl.ds(first + IN_ROWS * g, IN_ROWS)], buf.at[pl.ds(IN_ROWS * g, IN_ROWS)], sem.at[g]
        )
        for g in range(h // IN_ROWS)
    ]
    for copy in copies:
        copy.start()
    prepare()
    for q in range(h // OUT_ROWS):
        for i in range(OUT_ROWS):
            row = OUT_ROWS * q + i
            if row % IN_ROWS == 0:
                copies[row // IN_ROWS].wait()
            values = jnp.dot(basis[...], buf[row], preferred_element_type=F32)
            banded[64 * i : 64 * (i + 1), :] = values.astype(BF)
        terms = jnp.dot(banded[...], col[...], preferred_element_type=F32)
        for t in range(2):
            stage[t] = terms[:, 128 * t : 128 * (t + 1)]
        at = slice(OUT_ROWS * q, OUT_ROWS * (q + 1))
        for j in range(N):
            for r in range(RX):
                for t in range(2):
                    rows = stage[t, pl.ds(16 * j + r, OUT_ROWS, stride=64), :]
                    outs[j][r, at, 128 * t : 128 * (t + 1)] = rows.astype(outs[j].dtype)


def first_kernel(bt_hbm, col_hbm, pix_ref, *rest):
    outs, (basis, col, bt, buf, banded, stage, sem, bt_sem, col_sem) = rest[:N], rest[N:]
    bt_copy = pltpu.make_async_copy(bt_hbm, bt, bt_sem)
    col_copy = pltpu.make_async_copy(col_hbm, col, col_sem)
    bt_copy.start()
    col_copy.start()

    def prepare():
        x = lax.axis_index("x")
        basis[...] = jnp.zeros_like(basis)
        bt_copy.wait()
        for k in range(N):

            @pl.when(x == k)
            def _():
                for j in range(N):
                    at = RX * ((k + j) % N)
                    basis[16 * j : 16 * j + RX, :] = bt[at : at + RX, :]

        col_copy.wait()

    project_rows(0, basis, col, pix_ref, outs, buf, banded, stage, sem, prepare)


def second_kernel(first, basis, col, pix_ref, *rest):
    outs, (buf, banded, stage, sem) = rest[:N], rest[N:]
    project_rows(first, basis, col, pix_ref, outs, buf, banded, stage, sem, lambda: None)


ANY = pl.BlockSpec(memory_space=pl.ANY)


def project_specs(h, bands, c):
    terms = [jax.ShapeDtypeStruct((RX, h, R2), BF if j else F32) for j in range(N)]
    scratch = [
        pltpu.VMEM((h, bands, c), BF),
        pltpu.VMEM((64 * OUT_ROWS, c), BF),
        pltpu.VMEM((2, 64 * OUT_ROWS, R2 // 2), F32),
        pltpu.SemaphoreType.DMA((h // IN_ROWS,)),
    ]
    common = dict(
        compiler_params=params(48),
        cost_estimate=pl.CostEstimate(
            flops=2 * h * c * bands * 256, bytes_accessed=h * c * bands * 2, transcendentals=0
        ),
    )
    return terms, scratch, common


def project_first(bt, col, pix, h):
    _, bands, c = pix.shape
    terms, scratch, common = project_specs(h, bands, c)
    kept = [jax.ShapeDtypeStruct((64, bands), BF), jax.ShapeDtypeStruct(col.shape, BF)]
    out = pl.pallas_call(
        first_kernel,
        in_specs=[ANY] * 3,
        out_specs=[VMEM] * (N + 2),
        out_shape=terms + kept,
        scratch_shapes=[pltpu.VMEM(bt.shape, BF)] + scratch + [pltpu.SemaphoreType.DMA] * 2,
        name="project_first",
        **common,
    )(bt, col, pix)
    return list(out[:N]), out[N], out[N + 1]


def project_second(basis, col, pix, first, h):
    _, bands, c = pix.shape
    terms, scratch, common = project_specs(h, bands, c)
    return list(
        pl.pallas_call(
            functools.partial(second_kernel, first),
            in_specs=[VMEM, VMEM, ANY],
            out_specs=[VMEM] * N,
            out_shape=terms,
            scratch_shapes=scratch,
            name="project_second",
            **common,
        )(basis, col, pix)
    )


def collect_kernel(*refs):
    terms, out_ref = refs[:N], refs[N]
    for r in range(RX):
        total = sum(term[r].astype(F32) for term in terms)
        out_ref[:, R2 * r : R2 * (r + 1)] = total.astype(BF)


def collect(terms, flops):
    r, h, s = terms[0].shape
    return pl.pallas_call(
        collect_kernel,
        in_specs=[VMEM] * N,
        out_specs=VMEM,
        out_shape=jax.ShapeDtypeStruct((h, r * s), BF),
        compiler_params=params(8),
        cost_estimate=pl.CostEstimate(flops=flops, bytes_accessed=2 * 5 * r * h * s, transcendentals=0),
        name="collect",
    )(*terms)


def gram_kernel(zs, ys, early, late, *refs):
    outs, rhs = refs[:N], refs[N]
    x, y, core = lax.axis_index("x"), lax.axis_index("y"), lax.axis_index("core")
    n = zs.shape[0] // N
    for d in range(N):
        owner = lax.rem((1 - 2 * core) * (y - x) + d + N, N)
        theirs = (early, 0) if d in (0, 3) else (late, 2)
        for half, (block, base), e in ((core, (ys, 0), d), (1 - core, theirs, (N - d) % N)):
            e -= base
            at = pl.multiple_of((owner * 2 + half) * n, n)
            rhs[pl.ds(at, n), :] = block[n * e : n * (e + 1), :]
    for d in range(0, N, 2):
        pair = lax.dot_general(
            zs[...],
            rhs[2 * n * d : 2 * n * (d + 2), :],
            (((1,), (1,)), ((), ())),
            preferred_element_type=F32,
        )
        outs[d][...] = pair[:, : 2 * n]
        outs[d + 1][...] = pair[:, 2 * n :]


def gram(zs, ys, early, late):
    n, k = zs.shape
    return pl.pallas_call(
        gram_kernel,
        in_specs=[VMEM] * 4,
        out_specs=[VMEM] * N,
        out_shape=[jax.ShapeDtypeStruct((n, n // 2), F32)] * N,
        scratch_shapes=[pltpu.VMEM((2 * n, k), BF)],
        compiler_params=params(12),
        cost_estimate=pl.CostEstimate(
            flops=4 * n * n * k, bytes_accessed=2 * 3 * n * k, transcendentals=0
        ),
        name="gram",
    )(zs, ys, early, late)


def sum_kernel(g0, g1, g2, g3, *outs):
    n = outs[0].shape[0]
    for d in range(N):
        at = slice(n * d, n * (d + 1))
        outs[d][...] = (g0[at, :] + g1[at, :] + g2[at, :] + g3[at, :]) * SCALE


def sum_x(parts):
    n, m = parts[0].shape
    return pl.pallas_call(
        sum_kernel,
        in_specs=[VMEM] * N,
        out_specs=[VMEM] * N,
        out_shape=[jax.ShapeDtypeStruct((n // N, m), F32)] * N,
        compiler_params=params(2),
        name="sum_x",
    )(*parts)


def place_kernel(*refs):
    parts, out_ref = refs[:N], refs[N]
    z, core = lax.axis_index("z"), lax.axis_index("core")
    m = parts[0].shape[1]
    for d, part in zip(ORDER, parts):
        at = pl.multiple_of(lax.rem(z - (1 - 2 * core) * d + N, N) * m, m)
        out_ref[:, pl.ds(at, m)] = part[...]


def place(parts):
    n, m = parts[0].shape
    return pl.pallas_call(
        place_kernel,
        in_specs=[VMEM] * N,
        out_shape=jax.ShapeDtypeStruct((n, N * m), F32),
        compiler_params=params(2),
        name="place",
    )(*parts)


def spread(parts, axis):
    return [parts[0]] + [shift(parts[d], axis, d) for d in range(1, N)]


def local(pixels, band_basis, column_basis):
    pix, bt = pixels.transpose(0, 2, 1), band_basis.T
    h = pix.shape[0] // 2
    first, basis, col = project_first(bt, column_basis, pix, h)
    first = [first[0]] + [turn(first[j], j) for j in (1, 3, 2)]
    second = project_second(basis, col, pix, h, h)
    first, second[0] = lax.optimization_barrier((first, second[0]))
    second = [second[0]] + [turn(second[j], j) for j in (3, 1, 2)]
    mine = [collect(first, EARLY)]
    up = [[shift(mine[0], axis, -1)] for axis in "yz"]
    second, up = lax.optimization_barrier((second, up))
    mine.append(collect(second, LATE))
    for i, axis in enumerate("yz"):
        up[i].append(shift(mine[1], axis, -1))
    far = [shift(jnp.concatenate(up[i], axis=0), axis, -1) for i, axis in enumerate("yz")]
    down = [shift(jnp.concatenate(mine, axis=0), axis, 1) for axis in "yz"]
    early = swap(jnp.concatenate(mine + up[0], axis=0))
    early, far, down = lax.optimization_barrier((early, far, down))
    late = jnp.concatenate([far[0], down[0]], axis=0)
    ys = jnp.concatenate(mine + up[0] + [late], axis=0)
    zs = jnp.concatenate(mine + up[1] + [far[1], down[1]], axis=0)
    parts = spread(gram(zs, ys, early, swap(late)), "x")
    parts = sum_x([parts[d] for d in ORDER])
    parts = spread(parts, "z")
    return place([parts[d] for d in ORDER])


def solution(mesh):
    inner = Mesh(mesh.devices.reshape(4, 4, 2, 4), ("y", "z", "core", "x"))
    return jax.shard_map(
        local,
        mesh=inner,
        in_specs=(P(("y", "z", "core"), "x", None), P(), P("x", None)),
        out_specs=P(("y", "z", "core"), "x"),
        check_vma=False,
    )
```

```python
import functools

import jax
import jax.numpy as jnp
from jax import lax
from jax.experimental import pallas as pl
from jax.experimental.pallas import tpu as pltpu
from jax.sharding import Mesh, PartitionSpec as P

R3 = 48
R2 = 256
N = 4
RX = R3 // N
SCALE = 1.0 / (R3 * R2)
IN_ROWS = 8
OUT_ROWS = 16
EARLY = 20_000_000_000
LATE = 100_000_000
BF = jnp.bfloat16
F32 = jnp.float32
ORDER = (0, 2, 1, 3)
VMEM = pl.BlockSpec(memory_space=pltpu.VMEM)


def shift(v, axis, by):
    names = ("core", "x") if axis == "x" else (axis, "core")
    index = (lambda i, c: N * c + i) if axis == "x" else (lambda i, c: 2 * i + c)
    pairs = [(index(i, c), index((i + by * (1 - 2 * c)) % N, c)) for i in range(N) for c in range(2)]
    return lax.ppermute(v, names, pairs)


def turn(v, by):
    return lax.ppermute(v, "x", [(i, (i + by) % N) for i in range(N)])


def swap(v):
    return lax.ppermute(v, "core", [(0, 1), (1, 0)])


def params(mib):
    return pltpu.CompilerParams(vmem_limit_bytes=mib * 1024 * 1024)


def project_rows(first, basis, col, pix_ref, outs, buf, banded, stage, sem, prepare):
    h = outs[0].shape[1]
    copies = [
        pltpu.make_async_copy(
            pix_ref.at[pl.ds(first + IN_ROWS * g, IN_ROWS)], buf.at[pl.ds(IN_ROWS * g, IN_ROWS)], sem.at[g]
        )
        for g in range(h // IN_ROWS)
    ]
    for copy in copies:
        copy.start()
    prepare()
    for q in range(h // OUT_ROWS):
        for i in range(OUT_ROWS):
            row = OUT_ROWS * q + i
            if row % IN_ROWS == 0:
                copies[row // IN_ROWS].wait()
            values = jnp.dot(basis[...], buf[row], preferred_element_type=F32)
            banded[R3 * i : R3 * (i + 1), :] = values.astype(BF)
        terms = jnp.dot(banded[...], col[...], preferred_element_type=F32)
        for t in range(2):
            stage[t] = terms[:, 128 * t : 128 * (t + 1)]
        at = slice(OUT_ROWS * q, OUT_ROWS * (q + 1))
        for j in range(N):
            for r in range(RX):
                for t in range(2):
                    rows = stage[t, pl.ds(RX * j + r, OUT_ROWS, stride=R3), :]
                    outs[j][r, at, 128 * t : 128 * (t + 1)] = rows.astype(outs[j].dtype)


def first_kernel(bt_hbm, col_hbm, pix_ref, *rest):
    outs, (basis, col, bt, buf, banded, stage, sem, bt_sem, col_sem) = rest[:N], rest[N:]
    bt_copy = pltpu.make_async_copy(bt_hbm, bt, bt_sem)
    col_copy = pltpu.make_async_copy(col_hbm, col, col_sem)
    bt_copy.start()
    col_copy.start()

    def prepare():
        x = lax.axis_index("x")
        bt_copy.wait()
        for k in range(N):

            @pl.when(x == k)
            def _():
                rows = bt[...].astype(F32)
                turned = jnp.concatenate([rows[RX * k :], rows[: RX * k]], axis=0) if k else rows
                basis[...] = turned.astype(BF)

        col_copy.wait()

    project_rows(0, basis, col, pix_ref, outs, buf, banded, stage, sem, prepare)


def second_kernel(first, basis, col, pix_ref, *rest):
    outs, (buf, banded, stage, sem) = rest[:N], rest[N:]
    project_rows(first, basis, col, pix_ref, outs, buf, banded, stage, sem, lambda: None)


ANY = pl.BlockSpec(memory_space=pl.ANY)


def project_specs(h, bands, c):
    terms = [jax.ShapeDtypeStruct((RX, h, R2), BF if j else F32) for j in range(N)]
    scratch = [
        pltpu.VMEM((h, bands, c), BF),
        pltpu.VMEM((R3 * OUT_ROWS, c), BF),
        pltpu.VMEM((2, R3 * OUT_ROWS, R2 // 2), F32),
        pltpu.SemaphoreType.DMA((h // IN_ROWS,)),
    ]
    common = dict(
        compiler_params=params(48),
        cost_estimate=pl.CostEstimate(
            flops=2 * h * c * bands * 256, bytes_accessed=h * c * bands * 2, transcendentals=0
        ),
    )
    return terms, scratch, common


def project_first(bt, col, pix, h):
    _, bands, c = pix.shape
    terms, scratch, common = project_specs(h, bands, c)
    kept = [jax.ShapeDtypeStruct((R3, bands), BF), jax.ShapeDtypeStruct(col.shape, BF)]
    out = pl.pallas_call(
        first_kernel,
        in_specs=[ANY] * 3,
        out_specs=[VMEM] * (N + 2),
        out_shape=terms + kept,
        scratch_shapes=[pltpu.VMEM(bt.shape, BF)] + scratch + [pltpu.SemaphoreType.DMA] * 2,
        name="project_first",
        **common,
    )(bt, col, pix)
    return list(out[:N]), out[N], out[N + 1]


def project_second(basis, col, pix, first, h):
    _, bands, c = pix.shape
    terms, scratch, common = project_specs(h, bands, c)
    return list(
        pl.pallas_call(
            functools.partial(second_kernel, first),
            in_specs=[VMEM, VMEM, ANY],
            out_specs=[VMEM] * N,
            out_shape=terms,
            scratch_shapes=scratch,
            name="project_second",
            **common,
        )(basis, col, pix)
    )


def collect_kernel(*refs):
    terms, out_ref = refs[:N], refs[N]
    for r in range(RX):
        total = sum(term[r].astype(F32) for term in terms)
        out_ref[:, R2 * r : R2 * (r + 1)] = total.astype(BF)


def collect(terms, flops):
    r, h, s = terms[0].shape
    return pl.pallas_call(
        collect_kernel,
        in_specs=[VMEM] * N,
        out_specs=VMEM,
        out_shape=jax.ShapeDtypeStruct((h, r * s), BF),
        compiler_params=params(8),
        cost_estimate=pl.CostEstimate(flops=flops, bytes_accessed=2 * 5 * r * h * s, transcendentals=0),
        name="collect",
    )(*terms)


def gram_kernel(zs, ys, early, late, *refs):
    outs, rhs = refs[:N], refs[N]
    x, y, core = lax.axis_index("x"), lax.axis_index("y"), lax.axis_index("core")
    n = zs.shape[0] // N
    for d in range(N):
        owner = lax.rem((1 - 2 * core) * (y - x) + d + N, N)
        theirs = (early, 0) if d in (0, 3) else (late, 2)
        for half, (block, base), e in ((core, (ys, 0), d), (1 - core, theirs, (N - d) % N)):
            e -= base
            at = pl.multiple_of((owner * 2 + half) * n, n)
            rhs[pl.ds(at, n), :] = block[n * e : n * (e + 1), :]
    for d in range(0, N, 2):
        pair = lax.dot_general(
            zs[...],
            rhs[2 * n * d : 2 * n * (d + 2), :],
            (((1,), (1,)), ((), ())),
            preferred_element_type=F32,
        )
        outs[d][...] = pair[:, : 2 * n]
        outs[d + 1][...] = pair[:, 2 * n :]


def gram(zs, ys, early, late):
    n, k = zs.shape
    return pl.pallas_call(
        gram_kernel,
        in_specs=[VMEM] * 4,
        out_specs=[VMEM] * N,
        out_shape=[jax.ShapeDtypeStruct((n, n // 2), F32)] * N,
        scratch_shapes=[pltpu.VMEM((2 * n, k), BF)],
        compiler_params=params(12),
        cost_estimate=pl.CostEstimate(
            flops=4 * n * n * k, bytes_accessed=2 * 3 * n * k, transcendentals=0
        ),
        name="gram",
    )(zs, ys, early, late)


def sum_kernel(g0, g1, g2, g3, *outs):
    n = outs[0].shape[0]
    for d in range(N):
        at = slice(n * d, n * (d + 1))
        outs[d][...] = (g0[at, :] + g1[at, :] + g2[at, :] + g3[at, :]) * SCALE


def sum_x(parts):
    n, m = parts[0].shape
    return pl.pallas_call(
        sum_kernel,
        in_specs=[VMEM] * N,
        out_specs=[VMEM] * N,
        out_shape=[jax.ShapeDtypeStruct((n // N, m), F32)] * N,
        compiler_params=params(2),
        name="sum_x",
    )(*parts)


def place_kernel(*refs):
    parts, out_ref = refs[:N], refs[N]
    z, core = lax.axis_index("z"), lax.axis_index("core")
    m = parts[0].shape[1]
    for d, part in zip(ORDER, parts):
        at = pl.multiple_of(lax.rem(z - (1 - 2 * core) * d + N, N) * m, m)
        out_ref[:, pl.ds(at, m)] = part[...]


def place(parts):
    n, m = parts[0].shape
    return pl.pallas_call(
        place_kernel,
        in_specs=[VMEM] * N,
        out_shape=jax.ShapeDtypeStruct((n, N * m), F32),
        compiler_params=params(2),
        name="place",
    )(*parts)


def spread(parts, axis):
    return [parts[0]] + [shift(parts[d], axis, d) for d in range(1, N)]


def local(pixels, band_basis, column_basis):
    pix, bt = pixels.transpose(0, 2, 1), band_basis.T
    h = pix.shape[0] // 2
    first, basis, col = project_first(bt, column_basis, pix, h)
    first = [first[0]] + [turn(first[j], j) for j in (1, 3, 2)]
    second = project_second(basis, col, pix, h, h)
    first, second[0] = lax.optimization_barrier((first, second[0]))
    second = [second[0]] + [turn(second[j], j) for j in (3, 1, 2)]
    mine = [collect(first, EARLY)]
    up = [[shift(mine[0], axis, -1)] for axis in "yz"]
    second, up = lax.optimization_barrier((second, up))
    mine.append(collect(second, LATE))
    for i, axis in enumerate("yz"):
        up[i].append(shift(mine[1], axis, -1))
    far = [shift(jnp.concatenate(up[i], axis=0), axis, -1) for i, axis in enumerate("yz")]
    down = [shift(jnp.concatenate(mine, axis=0), axis, 1) for axis in "yz"]
    early = swap(jnp.concatenate(mine + up[0], axis=0))
    early, far, down = lax.optimization_barrier((early, far, down))
    late = jnp.concatenate([far[0], down[0]], axis=0)
    ys = jnp.concatenate(mine + up[0] + [late], axis=0)
    zs = jnp.concatenate(mine + up[1] + [far[1], down[1]], axis=0)
    parts = spread(gram(zs, ys, early, swap(late)), "x")
    parts = sum_x([parts[d] for d in ORDER])
    parts = spread(parts, "z")
    return place([parts[d] for d in ORDER])


def solution(mesh):
    inner = Mesh(mesh.devices.reshape(4, 4, 2, 4), ("y", "z", "core", "x"))
    return jax.shard_map(
        local,
        mesh=inner,
        in_specs=(P(("y", "z", "core"), "x", None), P(), P("x", None)),
        out_specs=P(("y", "z", "core"), "x"),
        check_vma=False,
    )
```
